32 devices in a mesh: replica: 4 (over y, x), fsdp: 8 (over z, core).
Axes of the slice: x: 2, y: 2, z: 4, core: 2. Of those that a mesh axis runs over, the one named last changes fastest.
Arguments:
- local_weights: bfloat16 [4, 512, 8192], P('replica', 'fsdp'), may hold values from -6 to 6
- base_weights: bfloat16 [512, 8192], P('fsdp'), may hold values from -6 to 6
- momentum: float32 [512, 8192], P('fsdp'), may hold values from -4 to 4
Outputs:
- fragment: bfloat16 [512, 8192], replicated
- new_momentum: float32 [512, 8192], P('fsdp')
The draws below stay inside these ranges and needn't reach their ends.
All inputs are finite; a program needn't handle non-finite values.
Results may differ from the reference program's by a relative error of at most 0.0053.
Values may be sent and summed in bfloat16 or wider, within the bound.
A program may use at most 128 MiB of HBM per device.

```python
import jax
import jax.numpy as jnp
from jax import lax

D = 8192
BLOCK = 128
ROWS = 512
REPLICAS = 4
N_REPLICA = 4


def block_scale(own_key, extent, shards, smallest, high):
    gain, own = 1.0, jax.random.fold_in(own_key, 6)
    for dim, blocks in shards:
        steps = jnp.exp(jax.random.uniform(jax.random.fold_in(own, dim), (blocks,), jnp.float32, smallest / len(shards), high / len(shards)))
        gain = gain * jnp.repeat(steps, extent[dim] // blocks).reshape([-1 if axis == dim else 1 for axis in range(len(extent))])
    return gain


def bell_draw(key, shape, width, most, split=(), dtype=jnp.bfloat16):
    drawn = jax.random.normal(key, shape, jnp.float32) * width
    if len(split) > 0:
        drawn = block_scale(key, shape, split, -0.22, 0.18) * drawn
    return jnp.clip(drawn, min=-most, max=most).astype(dtype)


def setup_inputs(seed: int = 0) -> dict:
    splits = jax.random.split(jax.random.key(seed), 4)
    return {
        "local_weights": bell_draw(splits[0], (REPLICAS, ROWS, D), 1.0, 6.0, ((0, 4), (1, 8))),
        "base_weights": bell_draw(splits[1], (ROWS, D), 1.0, 6.0, ((0, 8),)),
        "momentum": bell_draw(splits[2], (ROWS, D), 0.5, 4.0, ((0, 8),), jnp.float32),
    }


def quantize(base_weights, local_rows):
    delta = base_weights.astype(jnp.float32) - local_rows.astype(jnp.float32)
    blocks = delta.reshape(delta.shape[0], delta.shape[1] // BLOCK, BLOCK)
    largest = jnp.max(jnp.abs(blocks), axis=-1)
    scale = (largest / 448.0 + 1e-6).astype(jnp.bfloat16)
    scale_wide = lax.optimization_barrier(scale).astype(jnp.float32)
    codes = (blocks / scale_wide[..., None]).astype(jnp.bfloat16)
    return codes, scale


def dequantize(codes, scale):
    codes_wide = lax.optimization_barrier(codes).astype(jnp.float32)
    scale_wide = lax.optimization_barrier(scale).astype(jnp.float32)
    values = codes_wide * scale_wide[..., None]
    return values.reshape(values.shape[0], values.shape[1] * values.shape[2])


def reference(local_weights, base_weights, momentum):
    total = jnp.zeros(base_weights.shape, jnp.float32)
    for replica_id in range(N_REPLICA):
        codes, scale = quantize(base_weights, local_weights[replica_id])
        total = total + dequantize(codes, scale)
    pseudo = total / N_REPLICA
    new_momentum = 0.9 * momentum + pseudo
    fragment = (base_weights.astype(jnp.float32) - 0.7 * (pseudo + 0.9 * new_momentum)).astype(jnp.bfloat16)
    return fragment, new_momentum
```

```python
import functools

import jax
import jax.numpy as jnp
from jax import lax
from jax.experimental import pallas as pl
from jax.experimental.pallas import tpu as pltpu
from jax.sharding import PartitionSpec as P

block_width = 128
mesh_ids = pl.DeviceIdType.MESH

chunk_plan = (
    (2, "plane_ba"),
    (1, "plane_ab"),
    (1, "line_ba"),
    (2, "line_ab"),
    (2, "line_ba"),
)
chunk_units = 8


class Slots:
    def __init__(self):
        self.count = 0

    def take(self):
        self.count += 1
        return self.count - 1


def build_kernel(groups, shards, rows, width, chunks):
    outer, inner = 2, groups // 2
    depth = shards // 2
    send_slots, recv_slots = Slots(), Slots()

    def kernel(local_ref, base_ref, momentum_ref, frag_ref, moved_ref, parts, base_own, momentum_own, frag_own, moved_own, send_sem, recv_sem, local_sem):
        send_slots.count = recv_slots.count = 0
        r, f = lax.axis_index("replica"), lax.axis_index("fsdp")
        a, b = r // inner, r % inner
        z, c = f // 2, f % 2
        pending = []

        def device(a_, b_, z_, c_):
            return (a_ * inner + b_, z_ * 2 + c_)

        def send(src, dst, recv_slot, target, when=None):
            copy = pltpu.make_async_remote_copy(
                src_ref=src,
                dst_ref=dst,
                send_sem=send_sem.at[send_slots.take()],
                recv_sem=recv_sem.at[recv_slot],
                device_id=target,
                device_id_type=mesh_ids,
            )
            if when is None:
                copy.start()
            else:
                pl.when(when)(copy.start)
            pending.append((copy, when))

        def arrived(dst, recv_slot):
            pltpu.make_async_remote_copy(
                src_ref=dst,
                dst_ref=dst,
                send_sem=send_sem.at[0],
                recv_sem=recv_sem.at[recv_slot],
                device_id=(r, f),
                device_id_type=mesh_ids,
            ).wait_recv()

        barrier = pltpu.get_barrier_semaphore()
        for step in range(1, groups):
            pl.semaphore_signal(barrier, inc=1, device_id=(lax.rem(r + step, groups), f), device_id_type=mesh_ids)
        pl.semaphore_signal(barrier, inc=1, device_id=device(a, b, z, 1 - c), device_id_type=mesh_ids)

        @pl.when(z > 0)
        def _():
            pl.semaphore_signal(barrier, inc=1, device_id=device(a, b, z - 1, c), device_id_type=mesh_ids)

        @pl.when(z < depth - 1)
        def _():
            pl.semaphore_signal(barrier, inc=1, device_id=device(a, b, z + 1, c), device_id_type=mesh_ids)

        def columns(chunk, owner):
            start, size, _ = chunks[chunk]
            own = size // groups
            return pl.ds(pl.multiple_of(start + owner * own, 128), own)

        def own_columns(chunk):
            start, size, _ = chunks[chunk]
            return pl.ds(start // groups, size // groups)

        def local_copies(chunk):
            here, there = columns(chunk, r), own_columns(chunk)
            return (
                pltpu.make_async_copy(local_ref.at[0, :, here], parts.at[0, :, there], local_sem.at[chunk, 0]),
                pltpu.make_async_copy(base_ref.at[:, here], base_own.at[:, there], local_sem.at[chunk, 1]),
                pltpu.make_async_copy(momentum_ref.at[:, here], momentum_own.at[:, there], local_sem.at[chunk, 2]),
            )

        def result_copies(chunk):
            here, there = columns(chunk, r), own_columns(chunk)
            return (
                pltpu.make_async_copy(frag_own.at[:, there], frag_ref.at[z, c, :, here], local_sem.at[chunk, 3]),
                pltpu.make_async_copy(moved_own.at[:, there], moved_ref.at[:, here], local_sem.at[chunk, 4]),
            )

        for chunk in range(len(chunks)):
            for copy in local_copies(chunk):
                copy.start()
        pl.semaphore_wait(barrier, groups + jnp.where(z > 0, 1, 0) + jnp.where(z < depth - 1, 1, 0))

        scatter_slots = {}
        for chunk in range(len(chunks)):
            for step in range(1, groups):
                slot = scatter_slots[chunk, step] = recv_slots.take()
                owner = lax.rem(r + step, groups)
                send(local_ref.at[0, :, columns(chunk, owner)], parts.at[step, :, own_columns(chunk)], slot, (owner, f))

        def compute(chunk):
            for copy in local_copies(chunk):
                copy.wait()
            for step in range(1, groups):
                arrived(parts.at[step, :, own_columns(chunk)], scatter_slots[chunk, step])
            start, size, _ = chunks[chunk]

            def one_block(index, carry):
                cols = pl.ds(pl.multiple_of(start // groups + index * block_width, block_width), block_width)
                base = base_own[:, cols].astype(jnp.float32)
                total = jnp.zeros((rows, block_width), jnp.float32)
                for step in range(groups):
                    delta = base - parts[step, :, cols].astype(jnp.float32)
                    largest = jnp.max(jnp.abs(delta), axis=-1, keepdims=True)
                    scale = (largest / 448.0 + 1e-06).astype(jnp.bfloat16).astype(jnp.float32)
                    codes = (delta / scale).astype(jnp.bfloat16).astype(jnp.float32)
                    total = total + codes * scale
                pseudo = total / groups
                moved = 0.9 * momentum_own[:, cols] + pseudo
                moved_own[:, cols] = moved.astype(jnp.bfloat16)
                frag_own[:, cols] = (base - 0.7 * (pseudo + 0.9 * moved)).astype(jnp.bfloat16)
                return carry

            lax.fori_loop(0, size // groups // block_width, one_block, 0)
            for copy in result_copies(chunk):
                copy.start()

        def line_slots(length):
            ways = (1,) if length == 2 else (1, -1)
            return {(step, way): recv_slots.take() for step in range(1, length) for way in ways}

        def line_send(slots, step, place, length, neighbour, source, target, when=None):
            for way in (1, -1):
                if length == 2 and way == -1:
                    continue
                if length == 2:
                    send(source(place), target(place), slots[1, 1], neighbour(1 - place), when)
                    continue
                origin = place - way * (step - 1)
                to = place + way
                ok = (origin >= 0) & (origin < length) & (to >= 0) & (to < length)
                if when is not None:
                    ok = ok & when
                send(source(origin), target(origin), slots[step, way], neighbour(to), ok)

        def line_wait(slots, step, place, length, target, when=None):
            for way in (1, -1):
                if length == 2 and way == -1:
                    continue
                if length == 2:
                    origin, ok = 1 - place, when
                else:
                    origin = place - way * step
                    ok = (origin >= 0) & (origin < length)
                    if when is not None:
                        ok = ok & when
                if ok is None:
                    arrived(target(origin), slots[step, way])
                else:
                    pl.when(ok)(functools.partial(arrived, target(origin), slots[step, way]))

        def plane_gather(first, own, target, when=None):
            if first == "b":
                length1, place1, length2, place2 = inner, b, outer, a
                def at(p1, p2):
                    return target(p2, p1)
                def dev(p1, p2):
                    return device(p2, p1, z, c)
            else:
                length1, place1, length2, place2 = outer, a, inner, b
                def at(p1, p2):
                    return target(p1, p2)
                def dev(p1, p2):
                    return device(p1, p2, z, c)
            slots1 = line_slots(length1)
            slots2 = [line_slots(length2) for _ in range(length1)]

            line_send(slots1, 1, place1, length1, lambda p: dev(p, place2), lambda q: own, lambda q: at(q, place2), when)
            line_send(slots2[0], 1, place2, length2, lambda p: dev(place1, p), lambda q: own, lambda q: at(place1, q), when)
            yield
            for step in range(1, length1):
                line_wait(slots1, step, place1, length1, lambda q: at(q, place2), when)
                if step + 1 < length1:
                    line_send(slots1, step + 1, place1, length1, lambda p: dev(p, place2), lambda q: at(q, place2), lambda q: at(q, place2), when)
            for item in range(1, length1):
                p1 = lax.rem(place1 + item, length1)
                line_send(slots2[item], 1, place2, length2, lambda p: dev(place1, p), lambda q: at(p1, q), lambda q: at(p1, q), when)
            yield
            for item in range(length1):
                p1 = lax.rem(place1 + item, length1)
                for step in range(1, length2):
                    line_wait(slots2[item], step, place2, length2, lambda q: at(p1, q), when)
                    if step + 1 < length2:
                        line_send(slots2[item], step + 1, place2, length2, lambda p: dev(place1, p), lambda q: at(p1, q), lambda q: at(p1, q), when)

        def row_block(chunk, z_, c_):
            start, size, _ = chunks[chunk]
            return frag_ref.at[z_, c_, :, pl.ds(start, size)]

        def piece(chunk, z_):
            return lambda a_, b_: frag_ref.at[z_, c, :, columns(chunk, a_ * inner + b_)]

        def sibling_send(chunk, z_, slot, when=None):
            send(row_block(chunk, z_, c), row_block(chunk, z_, c), slot, device(a, b, z, 1 - c), when)

        def plane_first(chunk, first):
            own_source = frag_own.at[:, own_columns(chunk)]
            slots = line_slots(depth)
            sibling = {(0, 1): recv_slots.take()}
            for key in slots:
                sibling[key] = recv_slots.take()
            block = lambda q: row_block(chunk, q, c)
            step_z = lambda p: device(a, b, p, c)
            yield from plane_gather(first, own_source, piece(chunk, z))
            result_copies(chunk)[0].wait()
            line_send(slots, 1, z, depth, step_z, block, block)
            sibling_send(chunk, z, sibling[0, 1])
            yield
            for step in range(1, depth):
                line_wait(slots, step, z, depth, block)
                if step + 1 < depth:
                    line_send(slots, step + 1, z, depth, step_z, block, block)
                for way in (1, -1):
                    q = z - way * step
                    sibling_send(chunk, q, sibling[step, way], (q >= 0) & (q < depth))
                yield
            arrived(row_block(chunk, z, 1 - c), sibling[0, 1])
            for step in range(1, depth):
                for way in (1, -1):
                    q = z - way * step
                    pl.when((q >= 0) & (q < depth))(functools.partial(arrived, row_block(chunk, q, 1 - c), sibling[step, way]))

        def line_first(chunk, first):
            own_source = frag_own.at[:, own_columns(chunk)]
            slots = line_slots(depth)
            sibling = {(0, 1): recv_slots.take()}
            for key in slots:
                sibling[key] = recv_slots.take()
            own_piece = lambda q: piece(chunk, q)(a, b)
            step_z = lambda p: device(a, b, p, c)
            line_send(slots, 1, z, depth, step_z, lambda q: own_source, own_piece)
            gathers = [(plane_gather(first, own_source, piece(chunk, z)), z, (0, 1), None)]
            next(gathers[0][0])
            yield
            for step in range(1, depth):
                line_wait(slots, step, z, depth, own_piece)
                if step + 1 < depth:
                    line_send(slots, step + 1, z, depth, step_z, own_piece, own_piece)
                for way in (1, -1):
                    q = z - way * step
                    ok = (q >= 0) & (q < depth)
                    gather = plane_gather(first, own_piece(q), piece(chunk, q), ok)
                    next(gather)
                    gathers.append((gather, q, (step, way), ok))
                next(gathers[0][0] if step == 1 else gathers[2 * step - 3][0])
                if step > 1:
                    next(gathers[2 * step - 2][0])
                yield
            for gather in gathers[2 * depth - 3:]:
                next(gather[0])
            yield
            for index, (gather, q, key, ok) in enumerate(gathers):
                for _ in gather:
                    pass
                if index == 0:
                    result_copies(chunk)[0].wait()
                sibling_send(chunk, q, sibling[key], ok)
                if index % 2 == 0:
                    yield
            for _, q, key, ok in gathers:
                take = functools.partial(arrived, row_block(chunk, q, 1 - c), sibling[key])
                if ok is None:
                    take()
                else:
                    pl.when(ok)(take)

        def momentum_gather(chunk):
            target = lambda a_, b_: moved_ref.at[:, columns(chunk, a_ * inner + b_)]
            yield from plane_gather("ba"[chunk % 2], moved_own.at[:, own_columns(chunk)], target)
            result_copies(chunk)[1].wait()

        running = []

        def advance():
            for plan in list(running):
                try:
                    next(plan)
                except StopIteration:
                    running.remove(plan)

        later = []
        for chunk, (_, _, plan) in enumerate(chunks):
            compute(chunk)
            gather = plane_first if plan.startswith("plane") else line_first
            new = gather(chunk, plan[-2])
            next(new)
            advance()
            running.append(new)
            later.append(momentum_gather(chunk))
        for plan in later:
            next(plan)
        running.extend(later)
        while running:
            advance()
        for copy, when in pending:
            if when is None:
                copy.wait_send()
            else:
                pl.when(when)(copy.wait_send)

    return kernel, send_slots, recv_slots


def local(groups, shards, local_weights, base_weights, momentum):
    rows, width = base_weights.shape
    chunks, start = [], 0
    for units, plan in chunk_plan:
        size = units * (width // chunk_units)
        chunks.append((start, size, plan))
        start += size
    kernel, send_slots, recv_slots = build_kernel(groups, shards, rows, width, chunks)
    own = width // groups
    depth = shards // 2
    any_spec = pl.BlockSpec(memory_space=pl.ANY)

    def call(sends, receives):
        return pl.pallas_call(
            kernel,
            out_shape=(
                jax.ShapeDtypeStruct((depth, 2, rows, width), jnp.bfloat16),
                jax.ShapeDtypeStruct((rows, width), jnp.bfloat16),
            ),
            in_specs=[any_spec] * 3,
            out_specs=[any_spec] * 2,
            scratch_shapes=[
                pltpu.VMEM((groups, rows, own), jnp.bfloat16),
                pltpu.VMEM((rows, own), jnp.bfloat16),
                pltpu.VMEM((rows, own), jnp.float32),
                pltpu.VMEM((rows, own), jnp.bfloat16),
                pltpu.VMEM((rows, own), jnp.bfloat16),
                pltpu.SemaphoreType.DMA((sends,)),
                pltpu.SemaphoreType.DMA((receives,)),
                pltpu.SemaphoreType.DMA((len(chunks), 5)),
            ],
            compiler_params=pltpu.CompilerParams(collective_id=0, has_side_effects=True, vmem_limit_bytes=24 * 2**20),
        )

    jax.eval_shape(call(1024, 1024), local_weights, base_weights, momentum)
    fragment, moved = call(send_slots.count, recv_slots.count)(local_weights, base_weights, momentum)
    return fragment.reshape(shards * rows, width), moved.astype(jnp.float32)


def solution(mesh):
    return jax.shard_map(
        functools.partial(local, mesh.shape["replica"], mesh.shape["fsdp"]),
        mesh=mesh,
        in_specs=(P("replica", "fsdp", None), P("fsdp", None), P("fsdp", None)),
        out_specs=(P(), P("fsdp", None)),
        check_vma=False,
    )
```

```python
import functools

import jax
import jax.numpy as jnp
from jax import lax
from jax.experimental import pallas as pl
from jax.experimental.pallas import tpu as pltpu
from jax.sharding import PartitionSpec as P

block_width = 128
mesh_ids = pl.DeviceIdType.MESH

chunk_plan = (
    (2, "plane_ba"),
    (3, "line_ab"),
    (3, "line_ba"),
)
chunk_units = 8


class Slots:
    def __init__(self):
        self.count = 0

    def take(self):
        self.count += 1
        return self.count - 1


def build_kernel(groups, shards, rows, width, chunks):
    outer, inner = 2, groups // 2
    depth = shards // 2
    send_slots, recv_slots = Slots(), Slots()

    def kernel(local_ref, base_ref, momentum_ref, frag_ref, moved_ref, parts, base_own, momentum_own, frag_own, moved_own, send_sem, recv_sem, local_sem):
        send_slots.count = recv_slots.count = 0
        r, f = lax.axis_index("replica"), lax.axis_index("fsdp")
        a, b = r // inner, r % inner
        z, c = f // 2, f % 2
        pending = []

        def device(a_, b_, z_, c_):
            return (a_ * inner + b_, z_ * 2 + c_)

        def send(src, dst, recv_slot, target, when=None):
            copy = pltpu.make_async_remote_copy(
                src_ref=src,
                dst_ref=dst,
                send_sem=send_sem.at[send_slots.take()],
                recv_sem=recv_sem.at[recv_slot],
                device_id=target,
                device_id_type=mesh_ids,
            )
            if when is None:
                copy.start()
            else:
                pl.when(when)(copy.start)
            pending.append((copy, when))

        def arrived(dst, recv_slot):
            pltpu.make_async_remote_copy(
                src_ref=dst,
                dst_ref=dst,
                send_sem=send_sem.at[0],
                recv_sem=recv_sem.at[recv_slot],
                device_id=(r, f),
                device_id_type=mesh_ids,
            ).wait_recv()

        barrier = pltpu.get_barrier_semaphore()
        for step in range(1, groups):
            pl.semaphore_signal(barrier, inc=1, device_id=(lax.rem(r + step, groups), f), device_id_type=mesh_ids)
        pl.semaphore_signal(barrier, inc=1, device_id=device(a, b, z, 1 - c), device_id_type=mesh_ids)

        @pl.when(z > 0)
        def _():
            pl.semaphore_signal(barrier, inc=1, device_id=device(a, b, z - 1, c), device_id_type=mesh_ids)

        @pl.when(z < depth - 1)
        def _():
            pl.semaphore_signal(barrier, inc=1, device_id=device(a, b, z + 1, c), device_id_type=mesh_ids)

        def columns(chunk, owner):
            start, size, _ = chunks[chunk]
            own = size // groups
            return pl.ds(pl.multiple_of(start + owner * own, 128), own)

        def own_columns(chunk):
            start, size, _ = chunks[chunk]
            return pl.ds(start // groups, size // groups)

        def local_copies(chunk):
            here, there = columns(chunk, r), own_columns(chunk)
            return (
                pltpu.make_async_copy(local_ref.at[0, :, here], parts.at[0, :, there], local_sem.at[chunk, 0]),
                pltpu.make_async_copy(base_ref.at[:, here], base_own.at[:, there], local_sem.at[chunk, 1]),
                pltpu.make_async_copy(momentum_ref.at[:, here], momentum_own.at[:, there], local_sem.at[chunk, 2]),
            )

        def result_copies(chunk):
            here, there = columns(chunk, r), own_columns(chunk)
            return (
                pltpu.make_async_copy(frag_own.at[:, there], frag_ref.at[z, c, :, here], local_sem.at[chunk, 3]),
                pltpu.make_async_copy(moved_own.at[:, there], moved_ref.at[:, here], local_sem.at[chunk, 4]),
            )

        for chunk in range(len(chunks)):
            for copy in local_copies(chunk):
                copy.start()
        pl.semaphore_wait(barrier, groups + jnp.where(z > 0, 1, 0) + jnp.where(z < depth - 1, 1, 0))

        scatter_slots = {}
        for chunk in range(len(chunks)):
            for step in range(1, groups):
                slot = scatter_slots[chunk, step] = recv_slots.take()
                owner = lax.rem(r + step, groups)
                send(local_ref.at[0, :, columns(chunk, owner)], parts.at[step, :, own_columns(chunk)], slot, (owner, f))

        def compute(chunk):
            for copy in local_copies(chunk):
                copy.wait()
            for step in range(1, groups):
                arrived(parts.at[step, :, own_columns(chunk)], scatter_slots[chunk, step])
            start, size, _ = chunks[chunk]

            def one_block(index, carry):
                cols = pl.ds(pl.multiple_of(start // groups + index * block_width, block_width), block_width)
                base = base_own[:, cols].astype(jnp.float32)
                total = jnp.zeros((rows, block_width), jnp.float32)
                for step in range(groups):
                    delta = base - parts[step, :, cols].astype(jnp.float32)
                    largest = jnp.max(jnp.abs(delta), axis=-1, keepdims=True)
                    scale = (largest / 448.0 + 1e-06).astype(jnp.bfloat16).astype(jnp.float32)
                    codes = (delta / scale).astype(jnp.bfloat16).astype(jnp.float32)
                    total = total + codes * scale
                pseudo = total / groups
                moved = 0.9 * momentum_own[:, cols] + pseudo
                moved_own[:, cols] = moved.astype(jnp.bfloat16)
                frag_own[:, cols] = (base - 0.7 * (pseudo + 0.9 * moved)).astype(jnp.bfloat16)
                return carry

            lax.fori_loop(0, size // groups // block_width, one_block, 0)
            for copy in result_copies(chunk):
                copy.start()

        def line_slots(length):
            ways = (1,) if length == 2 else (1, -1)
            return {(step, way): recv_slots.take() for step in range(1, length) for way in ways}

        def line_send(slots, step, place, length, neighbour, source, target, when=None):
            for way in (1, -1):
                if length == 2 and way == -1:
                    continue
                if length == 2:
                    send(source(place), target(place), slots[1, 1], neighbour(1 - place), when)
                    continue
                origin = place - way * (step - 1)
                to = place + way
                ok = (origin >= 0) & (origin < length) & (to >= 0) & (to < length)
                if when is not None:
                    ok = ok & when
                send(source(origin), target(origin), slots[step, way], neighbour(to), ok)

        def line_wait(slots, step, place, length, target, when=None):
            for way in (1, -1):
                if length == 2 and way == -1:
                    continue
                if length == 2:
                    origin, ok = 1 - place, when
                else:
                    origin = place - way * step
                    ok = (origin >= 0) & (origin < length)
                    if when is not None:
                        ok = ok & when
                if ok is None:
                    arrived(target(origin), slots[step, way])
                else:
                    pl.when(ok)(functools.partial(arrived, target(origin), slots[step, way]))

        def plane_gather(first, own, target, when=None):
            if first == "b":
                length1, place1, length2, place2 = inner, b, outer, a
                def at(p1, p2):
                    return target(p2, p1)
                def dev(p1, p2):
                    return device(p2, p1, z, c)
            else:
                length1, place1, length2, place2 = outer, a, inner, b
                def at(p1, p2):
                    return target(p1, p2)
                def dev(p1, p2):
                    return device(p1, p2, z, c)
            slots1 = line_slots(length1)
            slots2 = [line_slots(length2) for _ in range(length1)]

            line_send(slots1, 1, place1, length1, lambda p: dev(p, place2), lambda q: own, lambda q: at(q, place2), when)
            line_send(slots2[0], 1, place2, length2, lambda p: dev(place1, p), lambda q: own, lambda q: at(place1, q), when)
            yield
            for step in range(1, length1):
                line_wait(slots1, step, place1, length1, lambda q: at(q, place2), when)
                if step + 1 < length1:
                    line_send(slots1, step + 1, place1, length1, lambda p: dev(p, place2), lambda q: at(q, place2), lambda q: at(q, place2), when)
            for item in range(1, length1):
                p1 = lax.rem(place1 + item, length1)
                line_send(slots2[item], 1, place2, length2, lambda p: dev(place1, p), lambda q: at(p1, q), lambda q: at(p1, q), when)
            yield
            for item in range(length1):
                p1 = lax.rem(place1 + item, length1)
                for step in range(1, length2):
                    line_wait(slots2[item], step, place2, length2, lambda q: at(p1, q), when)
                    if step + 1 < length2:
                        line_send(slots2[item], step + 1, place2, length2, lambda p: dev(place1, p), lambda q: at(p1, q), lambda q: at(p1, q), when)

        def row_block(chunk, z_, c_):
            start, size, _ = chunks[chunk]
            return frag_ref.at[z_, c_, :, pl.ds(start, size)]

        def piece(chunk, z_):
            return lambda a_, b_: frag_ref.at[z_, c, :, columns(chunk, a_ * inner + b_)]

        def sibling_send(chunk, z_, slot, when=None):
            send(row_block(chunk, z_, c), row_block(chunk, z_, c), slot, device(a, b, z, 1 - c), when)

        def plane_first(chunk, first):
            own_source = frag_own.at[:, own_columns(chunk)]
            slots = line_slots(depth)
            sibling = {(0, 1): recv_slots.take()}
            for key in slots:
                sibling[key] = recv_slots.take()
            block = lambda q: row_block(chunk, q, c)
            step_z = lambda p: device(a, b, p, c)
            yield from plane_gather(first, own_source, piece(chunk, z))
            result_copies(chunk)[0].wait()
            line_send(slots, 1, z, depth, step_z, block, block)
            sibling_send(chunk, z, sibling[0, 1])
            yield
            for step in range(1, depth):
                line_wait(slots, step, z, depth, block)
                if step + 1 < depth:
                    line_send(slots, step + 1, z, depth, step_z, block, block)
                for way in (1, -1):
                    q = z - way * step
                    sibling_send(chunk, q, sibling[step, way], (q >= 0) & (q < depth))
                yield
            arrived(row_block(chunk, z, 1 - c), sibling[0, 1])
            for step in range(1, depth):
                for way in (1, -1):
                    q = z - way * step
                    pl.when((q >= 0) & (q < depth))(functools.partial(arrived, row_block(chunk, q, 1 - c), sibling[step, way]))

        def line_first(chunk, first):
            own_source = frag_own.at[:, own_columns(chunk)]
            slots = line_slots(depth)
            sibling = {(0, 1): recv_slots.take()}
            for key in slots:
                sibling[key] = recv_slots.take()
            own_piece = lambda q: piece(chunk, q)(a, b)
            step_z = lambda p: device(a, b, p, c)
            line_send(slots, 1, z, depth, step_z, lambda q: own_source, own_piece)
            gathers = [(plane_gather(first, own_source, piece(chunk, z)), z, (0, 1), None)]
            next(gathers[0][0])
            yield
            for step in range(1, depth):
                line_wait(slots, step, z, depth, own_piece)
                if step + 1 < depth:
                    line_send(slots, step + 1, z, depth, step_z, own_piece, own_piece)
                for way in (1, -1):
                    q = z - way * step
                    ok = (q >= 0) & (q < depth)
                    gather = plane_gather(first, own_piece(q), piece(chunk, q), ok)
                    next(gather)
                    gathers.append((gather, q, (step, way), ok))
                next(gathers[0][0] if step == 1 else gathers[2 * step - 3][0])
                if step > 1:
                    next(gathers[2 * step - 2][0])
                yield
            for gather in gathers[2 * depth - 3:]:
                next(gather[0])
            yield
            for index, (gather, q, key, ok) in enumerate(gathers):
                for _ in gather:
                    pass
                if index == 0:
                    result_copies(chunk)[0].wait()
                sibling_send(chunk, q, sibling[key], ok)
                if index % 2 == 0:
                    yield
            for _, q, key, ok in gathers:
                take = functools.partial(arrived, row_block(chunk, q, 1 - c), sibling[key])
                if ok is None:
                    take()
                else:
                    pl.when(ok)(take)

        def momentum_gather(chunk):
            target = lambda a_, b_: moved_ref.at[:, columns(chunk, a_ * inner + b_)]
            yield from plane_gather("ba"[chunk % 2], moved_own.at[:, own_columns(chunk)], target)
            result_copies(chunk)[1].wait()

        running = []

        def advance():
            for plan in list(running):
                try:
                    next(plan)
                except StopIteration:
                    running.remove(plan)

        later = []
        for chunk, (_, _, plan) in enumerate(chunks):
            compute(chunk)
            gather = plane_first if plan.startswith("plane") else line_first
            new = gather(chunk, plan[-2])
            next(new)
            advance()
            running.append(new)
            later.append(momentum_gather(chunk))
        for plan in later:
            next(plan)
        running.extend(later)
        while running:
            advance()
        for copy, when in pending:
            if when is None:
                copy.wait_send()
            else:
                pl.when(when)(copy.wait_send)

    return kernel, send_slots, recv_slots


def local(groups, shards, local_weights, base_weights, momentum):
    rows, width = base_weights.shape
    chunks, start = [], 0
    for units, plan in chunk_plan:
        size = units * (width // chunk_units)
        chunks.append((start, size, plan))
        start += size
    kernel, send_slots, recv_slots = build_kernel(groups, shards, rows, width, chunks)
    own = width // groups
    depth = shards // 2
    any_spec = pl.BlockSpec(memory_space=pl.ANY)

    def call(sends, receives):
        return pl.pallas_call(
            kernel,
            out_shape=(
                pltpu.VMEM((depth, 2, rows, width), jnp.bfloat16),
                jax.ShapeDtypeStruct((rows, width), jnp.bfloat16),
            ),
            in_specs=[any_spec] * 3,
            out_specs=[pl.BlockSpec(memory_space=pltpu.VMEM), any_spec],
            scratch_shapes=[
                pltpu.VMEM((groups, rows, own), jnp.bfloat16),
                pltpu.VMEM((rows, own), jnp.bfloat16),
                pltpu.VMEM((rows, own), jnp.float32),
                pltpu.VMEM((rows, own), jnp.bfloat16),
                pltpu.VMEM((rows, own), jnp.bfloat16),
                pltpu.SemaphoreType.DMA((sends,)),
                pltpu.SemaphoreType.DMA((receives,)),
                pltpu.SemaphoreType.DMA((len(chunks), 5)),
            ],
            compiler_params=pltpu.CompilerParams(collective_id=0, has_side_effects=True, vmem_limit_bytes=58 * 2**20 - 2 * shards * rows * width),
        )

    jax.eval_shape(call(1024, 1024), local_weights, base_weights, momentum)
    fragment, moved = call(send_slots.count, recv_slots.count)(local_weights, base_weights, momentum)
    return fragment.reshape(shards * rows, width), moved.astype(jnp.float32)


def solution(mesh):
    return jax.shard_map(
        functools.partial(local, mesh.shape["replica"], mesh.shape["fsdp"]),
        mesh=mesh,
        in_specs=(P("replica", "fsdp", None), P("fsdp", None), P("fsdp", None)),
        out_specs=(P(), P("fsdp", None)),
        check_vma=False,
    )
```

```python
import functools

import jax
import jax.numpy as jnp
from jax import lax
from jax.experimental import pallas as pl
from jax.experimental.pallas import tpu as pltpu
from jax.sharding import PartitionSpec as P

block_width = 128
mesh_ids = pl.DeviceIdType.MESH

chunk_plan = (
    (2, "plane_ba"),
    (3, "line_ab"),
    (3, "line_ba"),
)
chunk_units = 8


class Slots:
    def __init__(self):
        self.count = 0

    def take(self):
        self.count += 1
        return self.count - 1


def build_kernel(groups, shards, rows, width, chunks):
    outer, inner = 2, groups // 2
    depth = shards // 2
    send_slots, recv_slots = Slots(), Slots()

    def kernel(local_ref, base_ref, momentum_ref, frag_ref, moved_ref, parts, base_own, momentum_own, frag_own, moved_own, send_sem, recv_sem, local_sem):
        send_slots.count = recv_slots.count = 0
        r, f = lax.axis_index("replica"), lax.axis_index("fsdp")
        a, b = r // inner, r % inner
        z, c = f // 2, f % 2
        pending = []

        def device(a_, b_, z_, c_):
            return (a_ * inner + b_, z_ * 2 + c_)

        def send(src, dst, recv_slot, target, when=None):
            copy = pltpu.make_async_remote_copy(
                src_ref=src,
                dst_ref=dst,
                send_sem=send_sem.at[send_slots.take()],
                recv_sem=recv_sem.at[recv_slot],
                device_id=target,
                device_id_type=mesh_ids,
            )
            if when is None:
                copy.start()
            else:
                pl.when(when)(copy.start)
            pending.append((copy, when))

        def arrived(dst, recv_slot):
            pltpu.make_async_remote_copy(
                src_ref=dst,
                dst_ref=dst,
                send_sem=send_sem.at[0],
                recv_sem=recv_sem.at[recv_slot],
                device_id=(r, f),
                device_id_type=mesh_ids,
            ).wait_recv()

        barrier = pltpu.get_barrier_semaphore()
        for step in range(1, groups):
            pl.semaphore_signal(barrier, inc=1, device_id=(lax.rem(r + step, groups), f), device_id_type=mesh_ids)
        pl.semaphore_signal(barrier, inc=1, device_id=device(a, b, z, 1 - c), device_id_type=mesh_ids)

        @pl.when(z > 0)
        def _():
            pl.semaphore_signal(barrier, inc=1, device_id=device(a, b, z - 1, c), device_id_type=mesh_ids)

        @pl.when(z < depth - 1)
        def _():
            pl.semaphore_signal(barrier, inc=1, device_id=device(a, b, z + 1, c), device_id_type=mesh_ids)

        def columns(chunk, owner):
            start, size, _ = chunks[chunk]
            own = size // groups
            return pl.ds(pl.multiple_of(start + owner * own, 128), own)

        def own_columns(chunk):
            start, size, _ = chunks[chunk]
            return pl.ds(start // groups, size // groups)

        def local_copies(chunk):
            here, there = columns(chunk, r), own_columns(chunk)
            return (
                pltpu.make_async_copy(local_ref.at[0, :, here], parts.at[0, :, there], local_sem.at[chunk, 0]),
                pltpu.make_async_copy(base_ref.at[:, here], base_own.at[:, there], local_sem.at[chunk, 1]),
                pltpu.make_async_copy(momentum_ref.at[:, here], momentum_own.at[:, there], local_sem.at[chunk, 2]),
            )

        def result_copies(chunk):
            here, there = columns(chunk, r), own_columns(chunk)
            return (
                pltpu.make_async_copy(frag_own.at[:, there], frag_ref.at[z, c, :, here], local_sem.at[chunk, 3]),
                pltpu.make_async_copy(moved_own.at[:, there], moved_ref.at[:, here], local_sem.at[chunk, 4]),
            )

        for chunk in range(len(chunks)):
            for copy in local_copies(chunk):
                copy.start()
        pl.semaphore_wait(barrier, groups + jnp.where(z > 0, 1, 0) + jnp.where(z < depth - 1, 1, 0))

        scatter_slots = {}
        for chunk in range(len(chunks)):
            for step in range(1, groups):
                slot = scatter_slots[chunk, step] = recv_slots.take()
                owner = lax.rem(r + step, groups)
                send(local_ref.at[0, :, columns(chunk, owner)], parts.at[step, :, own_columns(chunk)], slot, (owner, f))

        def compute(chunk):
            for copy in local_copies(chunk):
                copy.wait()
            for step in range(1, groups):
                arrived(parts.at[step, :, own_columns(chunk)], scatter_slots[chunk, step])
            start, size, _ = chunks[chunk]

            def one_block(index, carry):
                cols = pl.ds(pl.multiple_of(start // groups + index * block_width, block_width), block_width)
                base = base_own[:, cols].astype(jnp.float32)
                total = jnp.zeros((rows, block_width), jnp.float32)
                for step in range(groups):
                    delta = base - parts[step, :, cols].astype(jnp.float32)
                    largest = jnp.max(jnp.abs(delta), axis=-1, keepdims=True)
                    scale = (largest / 448.0 + 1e-06).astype(jnp.bfloat16).astype(jnp.float32)
                    codes = (delta / scale).astype(jnp.bfloat16).astype(jnp.float32)
                    total = total + codes * scale
                pseudo = total / groups
                moved = 0.9 * momentum_own[:, cols] + pseudo
                moved_own[:, cols] = moved.astype(jnp.bfloat16)
                frag_own[:, cols] = (base - 0.7 * (pseudo + 0.9 * moved)).astype(jnp.bfloat16)
                return carry

            lax.fori_loop(0, size // groups // block_width, one_block, 0)
            for copy in result_copies(chunk):
                copy.start()

        def line_slots(length):
            ways = (1,) if length == 2 else (1, -1)
            return {(step, way): recv_slots.take() for step in range(1, length) for way in ways}

        def line_send(slots, step, place, length, neighbour, source, target, when=None):
            for way in (1, -1):
                if length == 2 and way == -1:
                    continue
                if length == 2:
                    send(source(place), target(place), slots[1, 1], neighbour(1 - place), when)
                    continue
                origin = place - way * (step - 1)
                to = place + way
                ok = (origin >= 0) & (origin < length) & (to >= 0) & (to < length)
                if when is not None:
                    ok = ok & when
                send(source(origin), target(origin), slots[step, way], neighbour(to), ok)

        def line_wait(slots, step, place, length, target, when=None):
            for way in (1, -1):
                if length == 2 and way == -1:
                    continue
                if length == 2:
                    origin, ok = 1 - place, when
                else:
                    origin = place - way * step
                    ok = (origin >= 0) & (origin < length)
                    if when is not None:
                        ok = ok & when
                if ok is None:
                    arrived(target(origin), slots[step, way])
                else:
                    pl.when(ok)(functools.partial(arrived, target(origin), slots[step, way]))

        def plane_gather(first, own, target, when=None):
            if first == "b":
                length1, place1, length2, place2 = inner, b, outer, a
                def at(p1, p2):
                    return target(p2, p1)
                def dev(p1, p2):
                    return device(p2, p1, z, c)
            else:
                length1, place1, length2, place2 = outer, a, inner, b
                def at(p1, p2):
                    return target(p1, p2)
                def dev(p1, p2):
                    return device(p1, p2, z, c)
            slots1 = line_slots(length1)
            slots2 = [line_slots(length2) for _ in range(length1)]

            line_send(slots1, 1, place1, length1, lambda p: dev(p, place2), lambda q: own, lambda q: at(q, place2), when)
            line_send(slots2[0], 1, place2, length2, lambda p: dev(place1, p), lambda q: own, lambda q: at(place1, q), when)
            yield
            for step in range(1, length1):
                line_wait(slots1, step, place1, length1, lambda q: at(q, place2), when)
                if step + 1 < length1:
                    line_send(slots1, step + 1, place1, length1, lambda p: dev(p, place2), lambda q: at(q, place2), lambda q: at(q, place2), when)
            for item in range(1, length1):
                p1 = lax.rem(place1 + item, length1)
                line_send(slots2[item], 1, place2, length2, lambda p: dev(place1, p), lambda q: at(p1, q), lambda q: at(p1, q), when)
            yield
            for item in range(length1):
                p1 = lax.rem(place1 + item, length1)
                for step in range(1, length2):
                    line_wait(slots2[item], step, place2, length2, lambda q: at(p1, q), when)
                    if step + 1 < length2:
                        line_send(slots2[item], step + 1, place2, length2, lambda p: dev(place1, p), lambda q: at(p1, q), lambda q: at(p1, q), when)

        def row_block(chunk, z_, c_):
            start, size, _ = chunks[chunk]
            return frag_ref.at[z_, c_, :, pl.ds(start, size)]

        def piece(chunk, z_):
            return lambda a_, b_: frag_ref.at[z_, c, :, columns(chunk, a_ * inner + b_)]

        def sibling_send(chunk, z_, slot, when=None):
            send(row_block(chunk, z_, c), row_block(chunk, z_, c), slot, device(a, b, z, 1 - c), when)

        def plane_first(chunk, first):
            own_source = frag_own.at[:, own_columns(chunk)]
            slots = line_slots(depth)
            sibling = {(0, 1): recv_slots.take()}
            for key in slots:
                sibling[key] = recv_slots.take()
            block = lambda q: row_block(chunk, q, c)
            step_z = lambda p: device(a, b, p, c)
            yield from plane_gather(first, own_source, piece(chunk, z))
            result_copies(chunk)[0].wait()
            line_send(slots, 1, z, depth, step_z, block, block)
            sibling_send(chunk, z, sibling[0, 1])
            yield
            for step in range(1, depth):
                line_wait(slots, step, z, depth, block)
                if step + 1 < depth:
                    line_send(slots, step + 1, z, depth, step_z, block, block)
                for way in (1, -1):
                    q = z - way * step
                    sibling_send(chunk, q, sibling[step, way], (q >= 0) & (q < depth))
                yield
            arrived(row_block(chunk, z, 1 - c), sibling[0, 1])
            for step in range(1, depth):
                for way in (1, -1):
                    q = z - way * step
                    pl.when((q >= 0) & (q < depth))(functools.partial(arrived, row_block(chunk, q, 1 - c), sibling[step, way]))

        def line_first(chunk, first):
            own_source = frag_own.at[:, own_columns(chunk)]
            slots = line_slots(depth)
            sibling = {(0, 1): recv_slots.take()}
            for key in slots:
                sibling[key] = recv_slots.take()
            own_piece = lambda q: piece(chunk, q)(a, b)
            step_z = lambda p: device(a, b, p, c)
            line_send(slots, 1, z, depth, step_z, lambda q: own_source, own_piece)
            gathers = [(plane_gather(first, own_source, piece(chunk, z)), z, (0, 1), None)]
            next(gathers[0][0])
            yield
            for step in range(1, depth):
                line_wait(slots, step, z, depth, own_piece)
                if step + 1 < depth:
                    line_send(slots, step + 1, z, depth, step_z, own_piece, own_piece)
                for way in (1, -1):
                    q = z - way * step
                    ok = (q >= 0) & (q < depth)
                    gather = plane_gather(first, own_piece(q), piece(chunk, q), ok)
                    next(gather)
                    gathers.append((gather, q, (step, way), ok))
                next(gathers[0][0] if step == 1 else gathers[2 * step - 3][0])
                if step > 1:
                    next(gathers[2 * step - 2][0])
                yield
            for gather in gathers[2 * depth - 3:]:
                next(gather[0])
            yield
            for index, (gather, q, key, ok) in enumerate(gathers):
                for _ in gather:
                    pass
                if index == 0:
                    result_copies(chunk)[0].wait()
                sibling_send(chunk, q, sibling[key], ok)
                if index % 2 == 0:
                    yield
            for _, q, key, ok in gathers:
                take = functools.partial(arrived, row_block(chunk, q, 1 - c), sibling[key])
                if ok is None:
                    take()
                else:
                    pl.when(ok)(take)

        def momentum_gather(chunk):
            target = lambda a_, b_: moved_ref.at[:, columns(chunk, a_ * inner + b_)]
            yield from plane_gather("ba"[chunk % 2], moved_own.at[:, own_columns(chunk)], target)
            result_copies(chunk)[1].wait()

        running = []

        def advance():
            for plan in list(running):
                try:
                    next(plan)
                except StopIteration:
                    running.remove(plan)

        later = []
        for chunk, (_, _, plan) in enumerate(chunks):
            compute(chunk)
            gather = plane_first if plan.startswith("plane") else line_first
            new = gather(chunk, plan[-2])
            next(new)
            advance()
            running.insert(0, new)
            later.append(momentum_gather(chunk))
        for plan in later:
            next(plan)
        running.extend(later)
        while running:
            advance()
        for copy, when in pending:
            if when is None:
                copy.wait_send()
            else:
                pl.when(when)(copy.wait_send)

    return kernel, send_slots, recv_slots


def local(groups, shards, local_weights, base_weights, momentum):
    rows, width = base_weights.shape
    chunks, start = [], 0
    for units, plan in chunk_plan:
        size = units * (width // chunk_units)
        chunks.append((start, size, plan))
        start += size
    kernel, send_slots, recv_slots = build_kernel(groups, shards, rows, width, chunks)
    own = width // groups
    depth = shards // 2
    any_spec = pl.BlockSpec(memory_space=pl.ANY)

    def call(sends, receives):
        return pl.pallas_call(
            kernel,
            out_shape=(
                pltpu.VMEM((depth, 2, rows, width), jnp.bfloat16),
                jax.ShapeDtypeStruct((rows, width), jnp.bfloat16),
            ),
            in_specs=[any_spec] * 3,
            out_specs=[pl.BlockSpec(memory_space=pltpu.VMEM), any_spec],
            scratch_shapes=[
                pltpu.VMEM((groups, rows, own), jnp.bfloat16),
                pltpu.VMEM((rows, own), jnp.bfloat16),
                pltpu.VMEM((rows, own), jnp.float32),
                pltpu.VMEM((rows, own), jnp.bfloat16),
                pltpu.VMEM((rows, own), jnp.bfloat16),
                pltpu.SemaphoreType.DMA((sends,)),
                pltpu.SemaphoreType.DMA((receives,)),
                pltpu.SemaphoreType.DMA((len(chunks), 5)),
            ],
            compiler_params=pltpu.CompilerParams(collective_id=0, has_side_effects=True, vmem_limit_bytes=58 * 2**20 - 2 * shards * rows * width),
        )

    jax.eval_shape(call(1024, 1024), local_weights, base_weights, momentum)
    fragment, moved = call(send_slots.count, recv_slots.count)(local_weights, base_weights, momentum)
    return fragment.reshape(shards * rows, width), moved.astype(jnp.float32)


def solution(mesh):
    return jax.shard_map(
        functools.partial(local, mesh.shape["replica"], mesh.shape["fsdp"]),
        mesh=mesh,
        in_specs=(P("replica", "fsdp", None), P("fsdp", None), P("fsdp", None)),
        out_specs=(P(), P("fsdp", None)),
        check_vma=False,
    )
```

```python
import functools

import jax
import jax.numpy as jnp
from jax import lax
from jax.experimental import pallas as pl
from jax.experimental.pallas import tpu as pltpu
from jax.sharding import PartitionSpec as P

block_width = 128
mesh_ids = pl.DeviceIdType.MESH

chunk_plan = (
    (2, "plane_ba"),
    (3, "line_ab"),
    (3, "line_ba"),
)
chunk_units = 8


class Slots:
    def __init__(self):
        self.count = 0

    def take(self):
        self.count += 1
        return self.count - 1


def build_kernel(groups, shards, rows, width, chunks):
    outer, inner = 2, groups // 2
    depth = shards // 2
    send_slots, recv_slots = Slots(), Slots()

    def kernel(local_ref, base_ref, momentum_ref, frag_ref, moved_ref, parts, base_own, momentum_own, frag_own, moved_own, send_sem, recv_sem, local_sem):
        send_slots.count = recv_slots.count = 0
        r, f = lax.axis_index("replica"), lax.axis_index("fsdp")
        a, b = r // inner, r % inner
        z, c = f // 2, f % 2
        pending = []

        def device(a_, b_, z_, c_):
            return (a_ * inner + b_, z_ * 2 + c_)

        def send(src, dst, recv_slot, target, when=None):
            copy = pltpu.make_async_remote_copy(
                src_ref=src,
                dst_ref=dst,
                send_sem=send_sem.at[send_slots.take()],
                recv_sem=recv_sem.at[recv_slot],
                device_id=target,
                device_id_type=mesh_ids,
            )
            if when is None:
                copy.start()
            else:
                pl.when(when)(copy.start)
            pending.append((copy, when))

        def arrived(dst, recv_slot):
            pltpu.make_async_remote_copy(
                src_ref=dst,
                dst_ref=dst,
                send_sem=send_sem.at[0],
                recv_sem=recv_sem.at[recv_slot],
                device_id=(r, f),
                device_id_type=mesh_ids,
            ).wait_recv()

        barrier = pltpu.get_barrier_semaphore()
        for step in range(1, groups):
            pl.semaphore_signal(barrier, inc=1, device_id=(lax.rem(r + step, groups), f), device_id_type=mesh_ids)
        pl.semaphore_signal(barrier, inc=1, device_id=device(a, b, z, 1 - c), device_id_type=mesh_ids)

        @pl.when(z > 0)
        def _():
            pl.semaphore_signal(barrier, inc=1, device_id=device(a, b, z - 1, c), device_id_type=mesh_ids)

        @pl.when(z < depth - 1)
        def _():
            pl.semaphore_signal(barrier, inc=1, device_id=device(a, b, z + 1, c), device_id_type=mesh_ids)

        def columns(chunk, owner):
            start, size, _ = chunks[chunk]
            own = size // groups
            return pl.ds(pl.multiple_of(start + owner * own, 128), own)

        def own_columns(chunk):
            start, size, _ = chunks[chunk]
            return pl.ds(start // groups, size // groups)

        def local_copies(chunk):
            here, there = columns(chunk, r), own_columns(chunk)
            return (
                pltpu.make_async_copy(local_ref.at[0, :, here], parts.at[0, :, there], local_sem.at[chunk, 0]),
                pltpu.make_async_copy(base_ref.at[:, here], base_own.at[:, there], local_sem.at[chunk, 1]),
                pltpu.make_async_copy(momentum_ref.at[:, here], momentum_own.at[:, there], local_sem.at[chunk, 2]),
            )

        def result_copies(chunk):
            here, there = columns(chunk, r), own_columns(chunk)
            return (
                pltpu.make_async_copy(frag_own.at[:, there], frag_ref.at[z, c, :, here], local_sem.at[chunk, 3]),
                pltpu.make_async_copy(moved_own.at[:, there], moved_ref.at[:, here], local_sem.at[chunk, 4]),
            )

        for chunk in range(len(chunks)):
            for copy in local_copies(chunk):
                copy.start()
        pl.semaphore_wait(barrier, groups + jnp.where(z > 0, 1, 0) + jnp.where(z < depth - 1, 1, 0))

        scatter_slots = {}
        for chunk in range(len(chunks)):
            for step in range(1, groups):
                slot = scatter_slots[chunk, step] = recv_slots.take()
                owner = lax.rem(r + step, groups)
                send(local_ref.at[0, :, columns(chunk, owner)], parts.at[step, :, own_columns(chunk)], slot, (owner, f))

        def compute(chunk):
            for copy in local_copies(chunk):
                copy.wait()
            for step in range(1, groups):
                arrived(parts.at[step, :, own_columns(chunk)], scatter_slots[chunk, step])
            start, size, _ = chunks[chunk]

            def one_block(index, carry):
                cols = pl.ds(pl.multiple_of(start // groups + index * block_width, block_width), block_width)
                base = base_own[:, cols].astype(jnp.float32)
                total = jnp.zeros((rows, block_width), jnp.float32)
                for step in range(groups):
                    delta = base - parts[step, :, cols].astype(jnp.float32)
                    largest = jnp.max(jnp.abs(delta), axis=-1, keepdims=True)
                    scale = (largest / 448.0 + 1e-06).astype(jnp.bfloat16).astype(jnp.float32)
                    codes = (delta / scale).astype(jnp.bfloat16).astype(jnp.float32)
                    total = total + codes * scale
                pseudo = total / groups
                moved = 0.9 * momentum_own[:, cols] + pseudo
                moved_own[:, cols] = moved.astype(jnp.bfloat16)
                frag_own[:, cols] = (base - 0.7 * (pseudo + 0.9 * moved)).astype(jnp.bfloat16)
                return carry

            lax.fori_loop(0, size // groups // block_width, one_block, 0)
            for copy in result_copies(chunk):
                copy.start()

        def line_slots(length):
            ways = (1,) if length == 2 else (1, -1)
            return {(step, way): recv_slots.take() for step in range(1, length) for way in ways}

        def line_send(slots, step, place, length, neighbour, source, target, when=None):
            for way in (1, -1):
                if length == 2 and way == -1:
                    continue
                if length == 2:
                    send(source(place), target(place), slots[1, 1], neighbour(1 - place), when)
                    continue
                origin = place - way * (step - 1)
                to = place + way
                ok = (origin >= 0) & (origin < length) & (to >= 0) & (to < length)
                if when is not None:
                    ok = ok & when
                send(source(origin), target(origin), slots[step, way], neighbour(to), ok)

        def line_wait(slots, step, place, length, target, when=None):
            for way in (1, -1):
                if length == 2 and way == -1:
                    continue
                if length == 2:
                    origin, ok = 1 - place, when
                else:
                    origin = place - way * step
                    ok = (origin >= 0) & (origin < length)
                    if when is not None:
                        ok = ok & when
                if ok is None:
                    arrived(target(origin), slots[step, way])
                else:
                    pl.when(ok)(functools.partial(arrived, target(origin), slots[step, way]))

        def plane_gather(first, own, target, when=None):
            if first == "b":
                length1, place1, length2, place2 = inner, b, outer, a
                def at(p1, p2):
                    return target(p2, p1)
                def dev(p1, p2):
                    return device(p2, p1, z, c)
            else:
                length1, place1, length2, place2 = outer, a, inner, b
                def at(p1, p2):
                    return target(p1, p2)
                def dev(p1, p2):
                    return device(p1, p2, z, c)
            slots1 = line_slots(length1)
            slots2 = [line_slots(length2) for _ in range(length1)]

            line_send(slots1, 1, place1, length1, lambda p: dev(p, place2), lambda q: own, lambda q: at(q, place2), when)
            line_send(slots2[0], 1, place2, length2, lambda p: dev(place1, p), lambda q: own, lambda q: at(place1, q), when)
            yield
            for step in range(1, length1):
                line_wait(slots1, step, place1, length1, lambda q: at(q, place2), when)
                if step + 1 < length1:
                    line_send(slots1, step + 1, place1, length1, lambda p: dev(p, place2), lambda q: at(q, place2), lambda q: at(q, place2), when)
            for item in range(1, length1):
                p1 = lax.rem(place1 + item, length1)
                line_send(slots2[item], 1, place2, length2, lambda p: dev(place1, p), lambda q: at(p1, q), lambda q: at(p1, q), when)
            yield
            for item in range(length1):
                p1 = lax.rem(place1 + item, length1)
                for step in range(1, length2):
                    line_wait(slots2[item], step, place2, length2, lambda q: at(p1, q), when)
                    if step + 1 < length2:
                        line_send(slots2[item], step + 1, place2, length2, lambda p: dev(place1, p), lambda q: at(p1, q), lambda q: at(p1, q), when)

        def row_block(chunk, z_, c_):
            start, size, _ = chunks[chunk]
            return frag_ref.at[z_, c_, :, pl.ds(start, size)]

        def piece(chunk, z_):
            return lambda a_, b_: frag_ref.at[z_, c, :, columns(chunk, a_ * inner + b_)]

        def sibling_send(chunk, z_, slot, when=None):
            send(row_block(chunk, z_, c), row_block(chunk, z_, c), slot, device(a, b, z, 1 - c), when)

        def plane_first(chunk, first):
            own_source = frag_own.at[:, own_columns(chunk)]
            slots = line_slots(depth)
            sibling = {(0, 1): recv_slots.take()}
            for key in slots:
                sibling[key] = recv_slots.take()
            block = lambda q: row_block(chunk, q, c)
            step_z = lambda p: device(a, b, p, c)
            yield from plane_gather(first, own_source, piece(chunk, z))
            result_copies(chunk)[0].wait()
            line_send(slots, 1, z, depth, step_z, block, block)
            sibling_send(chunk, z, sibling[0, 1])
            yield
            for step in range(1, depth):
                line_wait(slots, step, z, depth, block)
                if step + 1 < depth:
                    line_send(slots, step + 1, z, depth, step_z, block, block)
                for way in (1, -1):
                    q = z - way * step
                    sibling_send(chunk, q, sibling[step, way], (q >= 0) & (q < depth))
                yield
            arrived(row_block(chunk, z, 1 - c), sibling[0, 1])
            for step in range(1, depth):
                for way in (1, -1):
                    q = z - way * step
                    pl.when((q >= 0) & (q < depth))(functools.partial(arrived, row_block(chunk, q, 1 - c), sibling[step, way]))

        def line_first(chunk, first):
            own_source = frag_own.at[:, own_columns(chunk)]
            slots = line_slots(depth)
            sibling = {(0, 1): recv_slots.take()}
            for key in slots:
                sibling[key] = recv_slots.take()
            own_piece = lambda q: piece(chunk, q)(a, b)
            step_z = lambda p: device(a, b, p, c)
            line_send(slots, 1, z, depth, step_z, lambda q: own_source, own_piece)
            gathers = [(plane_gather(first, own_source, piece(chunk, z)), z, (0, 1), None)]
            next(gathers[0][0])
            yield
            for step in range(1, depth):
                line_wait(slots, step, z, depth, own_piece)
                if step + 1 < depth:
                    line_send(slots, step + 1, z, depth, step_z, own_piece, own_piece)
                for way in (1, -1):
                    q = z - way * step
                    ok = (q >= 0) & (q < depth)
                    gather = plane_gather(first, own_piece(q), piece(chunk, q), ok)
                    next(gather)
                    gathers.append((gather, q, (step, way), ok))
                next(gathers[0][0] if step == 1 else gathers[2 * step - 3][0])
                if step > 1:
                    next(gathers[2 * step - 2][0])
                yield
            for gather in gathers[2 * depth - 3:]:
                next(gather[0])
            for index, (gather, q, key, ok) in enumerate(gathers):
                for _ in gather:
                    pass
                if index == 0:
                    result_copies(chunk)[0].wait()
                sibling_send(chunk, q, sibling[key], ok)
                if index % 2 == 0:
                    yield
            for _, q, key, ok in gathers:
                take = functools.partial(arrived, row_block(chunk, q, 1 - c), sibling[key])
                if ok is None:
                    take()
                else:
                    pl.when(ok)(take)

        def momentum_gather(chunk):
            target = lambda a_, b_: moved_ref.at[:, columns(chunk, a_ * inner + b_)]
            yield from plane_gather("ba"[chunk % 2], moved_own.at[:, own_columns(chunk)], target)
            result_copies(chunk)[1].wait()

        running = []

        def advance():
            for plan in list(running):
                try:
                    next(plan)
                except StopIteration:
                    running.remove(plan)

        later = []
        for chunk, (_, _, plan) in enumerate(chunks):
            compute(chunk)
            gather = plane_first if plan.startswith("plane") else line_first
            new = gather(chunk, plan[-2])
            next(new)
            advance()
            running.insert(0, new)
            later.append(momentum_gather(chunk))
        for plan in later:
            next(plan)
        running.extend(later)
        while running:
            advance()
        for copy, when in pending:
            if when is None:
                copy.wait_send()
            else:
                pl.when(when)(copy.wait_send)

    return kernel, send_slots, recv_slots


def local(groups, shards, local_weights, base_weights, momentum):
    rows, width = base_weights.shape
    chunks, start = [], 0
    for units, plan in chunk_plan:
        size = units * (width // chunk_units)
        chunks.append((start, size, plan))
        start += size
    kernel, send_slots, recv_slots = build_kernel(groups, shards, rows, width, chunks)
    own = width // groups
    depth = shards // 2
    any_spec = pl.BlockSpec(memory_space=pl.ANY)

    def call(sends, receives):
        return pl.pallas_call(
            kernel,
            out_shape=(
                pltpu.VMEM((depth, 2, rows, width), jnp.bfloat16),
                jax.ShapeDtypeStruct((rows, width), jnp.bfloat16),
            ),
            in_specs=[any_spec] * 3,
            out_specs=[pl.BlockSpec(memory_space=pltpu.VMEM), any_spec],
            scratch_shapes=[
                pltpu.VMEM((groups, rows, own), jnp.bfloat16),
                pltpu.VMEM((rows, own), jnp.bfloat16),
                pltpu.VMEM((rows, own), jnp.float32),
                pltpu.VMEM((rows, own), jnp.bfloat16),
                pltpu.VMEM((rows, own), jnp.bfloat16),
                pltpu.SemaphoreType.DMA((sends,)),
                pltpu.SemaphoreType.DMA((receives,)),
                pltpu.SemaphoreType.DMA((len(chunks), 5)),
            ],
            compiler_params=pltpu.CompilerParams(collective_id=0, has_side_effects=True, vmem_limit_bytes=58 * 2**20 - 2 * shards * rows * width),
        )

    jax.eval_shape(call(1024, 1024), local_weights, base_weights, momentum)
    fragment, moved = call(send_slots.count, recv_slots.count)(local_weights, base_weights, momentum)
    return fragment.reshape(shards * rows, width), moved.astype(jnp.float32)


def solution(mesh):
    return jax.shard_map(
        functools.partial(local, mesh.shape["replica"], mesh.shape["fsdp"]),
        mesh=mesh,
        in_specs=(P("replica", "fsdp", None), P("fsdp", None), P("fsdp", None)),
        out_specs=(P(), P("fsdp", None)),
        check_vma=False,
    )
```
